32 devices in a mesh: lon: 8 (over z, y), lat: 4 (over x, core).
Axes of the slice: x: 2, y: 2, z: 4, core: 2. Of those that a mesh axis runs over, the one named last changes fastest.
Arguments:
- tracers: float32 [2, 8, 768, 1024], P(None, None, 'lat', 'lon'), may hold values from -6 to 6
- zonal_velocity: float32 [8, 768, 1024], P(None, 'lat', 'lon'), may hold values from -0.4 to 0.4
- merid_velocity: float32 [8, 768, 1024], P(None, 'lat', 'lon'), may hold values from -0.4 to 0.4
- diffusivity: float32 [768, 1024], P('lat', 'lon'), may hold values from 0.02 to 0.2
- depth: int32 [768, 1024], P('lat', 'lon'), may hold values from 0 to 8, as said below
Outputs:
- tracers_out: float32 [2, 8, 768, 1024], P(None, None, 'lat', 'lon')
The draws below stay inside these ranges and needn't reach their ends.
Inputs may be any that keep to these rules, and one draw needn't show every extreme that they name: `depth`: row 0 is land everywhere, the top three rows have at least 4 wet levels, and some column has all 8 levels wet.
All inputs are finite; a program needn't handle non-finite values.
Results may differ from the reference program's by a relative error of at most 0.0003.
Values sent between devices are 32-bit elements; how exact they have to be, the bound alone decides.
A program may use at most 128 MiB of HBM per device.

```python
import math
import jax
import jax.numpy as jnp
from jax import lax

LEV = 8
TRACERS = 2
ITERS = 4
NX = 1024
NY = 768


def draw_depth(key, part):
    key_tile, key_cell = jax.random.split(jax.random.fold_in(key, 7))
    tiles_y = (NY + 15) // 16
    tiles_x = (NX + 15) // 16
    coarse = jax.random.randint(key_tile, (tiles_y, tiles_x), -4, LEV + 5)
    row_idx = lax.broadcasted_iota(jnp.int32, (NY, NX), 0)
    col_idx = lax.broadcasted_iota(jnp.int32, (NY, NX), 1)
    spread = coarse[row_idx // 16, col_idx // 16]
    fine = jax.random.randint(key_cell, (NY, NX), -2, 3)
    levels = jnp.clip(spread + fine, 0, LEV)
    levels = jnp.where(row_idx >= NY - 3, jnp.maximum(levels, LEV // 2), levels)
    levels = jnp.where(row_idx == 0, 0, levels)
    levels = jnp.where((row_idx == NY - 1) & (col_idx == 0), LEV, levels)
    return levels.astype(jnp.int32)


def shard_levels(stream_key, dims, shards, smallest, largest):
    level = 1.0
    for axis_at, shards_of in shards:
        draws = jax.random.uniform(jax.random.fold_in(jax.random.fold_in(stream_key, 6), axis_at), (shards_of,), jnp.float32, smallest / len(shards), largest / len(shards))
        level = level * jnp.repeat(jnp.exp(draws), dims[axis_at] // shards_of).reshape((-1,) + (1,) * (len(dims) - 1 - axis_at))
    return level


def normal_values(own_key, shape, width, limit, pieces=(), held_as=jnp.bfloat16):
    gain = shard_levels(own_key, shape, pieces, -0.22, 0.18) if pieces else 1.0
    entries = jax.random.normal(own_key, shape, jnp.float32) * width * gain
    return jnp.minimum(jnp.maximum(entries, -limit), limit).astype(held_as)


def setup_inputs(seed: int = 0) -> dict:
    key_of = jax.random.split(jax.random.key(seed), 6)
    return {
        "tracers": normal_values(key_of[0], (TRACERS, LEV, NY, NX), 1.0, 6.0, ((2, 4), (3, 8)), jnp.float32),
        "zonal_velocity": normal_values(key_of[1], (LEV, NY, NX), 0.1, 0.4, ((1, 4), (2, 8)), jnp.float32),
        "merid_velocity": normal_values(key_of[2], (LEV, NY, NX), 0.1, 0.4, ((1, 4), (2, 8)), jnp.float32),
        "diffusivity": jnp.clip(jnp.exp(math.log(0.2) - 2.3025851 * jax.random.uniform(key_of[3], (NY, NX), jnp.float32) ** shard_levels(key_of[3], (NY, NX), ((0, 4), (1, 8)), -0.2, 0.2)), 0.02, 0.2),
        "depth": draw_depth(jax.random.fold_in(key_of[5], 71), 0),
    }


def extend(field, sign):
    rows = field.shape[-2]
    ext = jnp.concatenate([field[..., -2:], field, field[..., :2]], axis=-1)
    top = jnp.flip(ext[..., rows - 3:rows - 1, :], axis=(-2, -1)) * sign
    bottom = jnp.zeros_like(ext[..., :2, :])
    return jnp.concatenate([bottom, ext, top], axis=-2)

def face_flux(q_m, q_a, q_b, q_n, vel_a, vel_b, kap_a, kap_b):
    kprod = kap_a * kap_b
    opened = jnp.where(kprod > 0, 1.0, 0.0).astype(jnp.float32)
    vel = 0.5 * (vel_a + vel_b) * opened
    curve_a = q_b - 2.0 * q_a + q_m
    curve_b = q_n - 2.0 * q_b + q_a
    return vel * (0.5 * (q_a + q_b) - (curve_a + curve_b) / 12.0) + jnp.abs(vel) * (curve_b - curve_a) / 12.0 - jnp.sqrt(kprod) * (q_b - q_a)

def tendency(padded, fpad):
    rows = padded.shape[-2] - 4
    cols = padded.shape[-1] - 4
    east_vel, north_vel, kappa = (fpad[0], fpad[1], fpad[2])
    qx = padded[..., 2:rows + 2, :]
    flux_x = face_flux(qx[..., 0:cols + 1], qx[..., 1:cols + 2], qx[..., 2:cols + 3], qx[..., 3:cols + 4], east_vel[:, 2:rows + 2, 1:cols + 2], east_vel[:, 2:rows + 2, 2:cols + 3], kappa[:, 2:rows + 2, 1:cols + 2], kappa[:, 2:rows + 2, 2:cols + 3])
    qy = padded[..., 2:cols + 2]
    flux_y = face_flux(qy[..., 0:rows + 1, :], qy[..., 1:rows + 2, :], qy[..., 2:rows + 3, :], qy[..., 3:rows + 4, :], north_vel[:, 1:rows + 2, 2:cols + 2], north_vel[:, 2:rows + 3, 2:cols + 2], kappa[:, 1:rows + 2, 2:cols + 2], kappa[:, 2:rows + 3, 2:cols + 2])
    return flux_x[..., 1:] - flux_x[..., :-1] + (flux_y[..., 1:, :] - flux_y[..., :-1, :])

def reference(tracers, zonal_velocity, merid_velocity, diffusivity, depth):
    levels = lax.broadcasted_iota(jnp.int32, zonal_velocity.shape, 0)
    wet = jnp.where(levels < depth[None], 1.0, 0.0).astype(jnp.float32)
    fields = jnp.stack([zonal_velocity * wet, merid_velocity * wet, diffusivity[None] * wet])
    signs = jnp.array([-1.0, -1.0, 1.0], jnp.float32).reshape(3, 1, 1, 1)
    fpad = extend(fields, signs)
    state = tracers * wet
    for step in range(ITERS):
        padded = extend(state, jnp.float32(1.0))
        state = (state - tendency(padded, fpad)) * wet
    return state
```

```python
import functools

import jax
import jax.numpy as jnp
from jax import lax
from jax.experimental import pallas as pl
from jax.experimental.pallas import tpu as pltpu
from jax.sharding import PartitionSpec as P

ITERS = 4
HALO = 2
CHUNKS = 4


def lanes_of():
    return lax.broadcasted_iota(jnp.int32, (8, 128), 1)


def pack_edges(tiles):
    lane = lanes_of()
    span = 4
    while len(tiles) > 1:
        keep = (lane >= 126) | (lane < span - 2)
        tiles = [
            jnp.where(keep, tiles[i], pltpu.roll(tiles[i + 1], span, 1))
            for i in range(0, len(tiles), 2)
        ]
        span *= 2
    return tiles[0]


def turn(tile, slot):
    shift = (-4 * slot) % 128
    return pltpu.roll(tile, shift, 1) if shift else tile


def mirrored(tile):
    return jnp.take_along_axis(tile, 127 - lanes_of(), axis=1)


def face(vel_a, vel_b, root_a, root_b):
    root = root_a * root_b
    v = jnp.where(root > 0, (vel_a + vel_b) * (1.0 / 24.0), 0.0)
    w = jnp.abs(v)
    g = 3.0 * w + root
    v7 = 7.0 * v
    return -(v + w), v7 + g, v7 - g, w - v


def kernel(
    lons, lats, rows, levels, comps,
    tr, zu, mv, kap, dep, out,
    q, uk, vk, coef, snd, rcv_w, rcv_e, stage, res, kap_v, dep_v,
    lon_send, lon_recv, lat_send, lat_recv, in_sem, out_sem,
):
    lon, lat = lax.axis_index("lon"), lax.axis_index("lat")
    west = {"lon": lax.rem(lon + lons - 1, lons), "lat": lat}
    east = {"lon": lax.rem(lon + 1, lons), "lat": lat}
    south = {"lon": lon, "lat": lat - 1}
    north = {"lon": lon, "lat": lat + 1}
    mirror = {"lon": lons - 1 - lon, "lat": lat}
    inner, top = lat > 0, lat == lats - 1
    below_top = lat < lats - 1
    block = 32 // comps
    blocks = rows // block
    per = blocks // CHUNKS
    order = [0, CHUNKS - 1] + list(range(1, CHUNKS - 1))
    lane = lanes_of()
    level = lax.broadcasted_iota(jnp.int32, (8, 128), 0)
    first, last = lane == 0, lane == 127
    first_two, last_two = lane < HALO, lane >= 128 - HALO

    loads_f = [
        pltpu.make_async_copy(kap, kap_v, in_sem.at[0]),
        pltpu.make_async_copy(dep, dep_v, in_sem.at[1]),
    ]
    for l in range(levels):
        span = pl.ds(l * rows, rows)
        loads_f.append(pltpu.make_async_copy(zu.at[span], uk.at[:, 0, l], in_sem.at[2 + l]))
        loads_f.append(
            pltpu.make_async_copy(
                mv.at[span], vk.at[pl.ds(HALO, rows), 0, l], in_sem.at[2 + levels + l]
            )
        )
    loads_q = []
    for c in range(comps):
        for l in range(levels):
            loads_q.append(
                pltpu.make_async_copy(
                    tr.at[pl.ds((c * levels + l) * rows, rows)],
                    q.at[0, pl.ds(HALO, rows), c, l],
                    in_sem.at[2 + 2 * levels + c * levels + l],
                )
            )
    for copy in loads_f + loads_q:
        copy.start()

    barrier = pltpu.get_barrier_semaphore()

    def greet(device):
        pl.semaphore_signal(barrier, inc=1, device_id=device, device_id_type=pl.DeviceIdType.MESH)

    greet(west)
    greet(east)
    pl.when(inner)(lambda: greet(south))
    pl.when(below_top)(lambda: greet(north))
    pl.when(top)(lambda: greet(mirror))

    def remote(src, dst, send, recv, device):
        return pltpu.make_async_remote_copy(
            src_ref=src, dst_ref=dst, send_sem=send, recv_sem=recv,
            device_id=device, device_id_type=pl.DeviceIdType.MESH,
        )

    def lon_copies(e, ch):
        span = pl.ds(ch * per, per)
        src = snd.at[e, span]
        return (
            remote(src, rcv_e.at[e, span], lon_send.at[e, ch, 0], lon_recv.at[e, ch, 0], west),
            remote(src, rcv_w.at[e, span], lon_send.at[e, ch, 1], lon_recv.at[e, ch, 1], east),
        )

    def down_copy(e, arr):
        return remote(
            arr.at[pl.ds(HALO, HALO)], arr.at[pl.ds(rows + HALO, HALO)],
            lat_send.at[e, 0], lat_recv.at[e, 1], south,
        )

    def up_copy(e, arr):
        return remote(
            arr.at[pl.ds(rows, HALO)], arr.at[pl.ds(0, HALO)],
            lat_send.at[e, 1], lat_recv.at[e, 0], north,
        )

    def fold_copy(e, arr):
        return remote(
            stage.at[e], arr.at[pl.ds(rows + HALO, HALO)],
            lat_send.at[e, 1], lat_recv.at[e, 1], mirror,
        )

    def send_down(e, arr):
        pl.when(inner)(lambda: down_copy(e, arr).start())

    def send_up(e, arr, signs):
        pl.when(below_top)(lambda: up_copy(e, arr).start())

        @pl.when(top)
        def _():
            for j in range(HALO):
                for c in range(comps):
                    stage[e, j, c] = mirrored(arr[rows - j, c]) * signs[c]
            fold_copy(e, arr).start()

    def send_lon(e, ch):
        for copy in lon_copies(e, ch):
            copy.start()

    def wait_lon(e, ch):
        for copy in lon_copies(e, ch):
            copy.wait_recv()

    def wait_low(e, arr):
        pl.when(inner)(lambda: up_copy(e, arr).wait_recv())

    def wait_high(e, arr):
        fold_copy(e, arr).wait_recv()

    def wait_sends(e, arr):
        for ch in range(CHUNKS):
            for copy in lon_copies(e, ch):
                copy.wait_send()
        pl.when(inner)(lambda: down_copy(e, arr).wait_send())
        fold_copy(e, arr).wait_send()

    def incoming(e, b):
        return jnp.where((lane & 2) != 0, rcv_w[e, b], rcv_e[e, b])

    def over(ch, body):
        def step(b, carry):
            body(b)
            return carry

        lax.fori_loop(ch * per, (ch + 1) * per, step, 0)

    @pl.when(lat == 0)
    def _():
        zero = jnp.zeros((HALO, comps, 8, 128), jnp.float32)
        vk[pl.ds(0, HALO)] = zero
        for k in range(ITERS):
            q[k, pl.ds(0, HALO)] = zero

    for copy in loads_f:
        copy.wait()

    def build_fields(b):
        tiles = []
        for i in range(block):
            r = b * block + i
            wet = level < dep_v[pl.ds(r, 1), :]
            kw = jnp.where(wet, jnp.sqrt(kap_v[pl.ds(r, 1), :]), 0.0)
            uk[r, 1] = kw
            vk[r + HALO, 1] = kw
            tiles += [uk[r, 0], kw]
        snd[ITERS, b] = pack_edges(tiles)

    neighbours = 3 + inner.astype(jnp.int32)
    for n, ch in enumerate(order):
        over(ch, build_fields)
        if n == 0:
            pl.semaphore_wait(barrier, neighbours)
        send_lon(ITERS, ch)
        if ch == 0:
            send_down(ITERS, vk)
        if ch == CHUNKS - 1:
            send_up(ITERS, vk, (-1.0, 1.0))

    for copy in loads_q:
        copy.wait()

    def build_state(b):
        tiles = []
        for i in range(block):
            r = b * block + i
            wet = level < dep_v[pl.ds(r, 1), :]
            for c in range(comps):
                tile = jnp.where(wet, q[0, r + HALO, c], 0.0)
                q[0, r + HALO, c] = tile
                tiles.append(tile)
        snd[0, b] = pack_edges(tiles)

    for ch in order:
        over(ch, build_state)
        send_lon(0, ch)
        if ch == 0:
            send_down(0, q.at[0])
        if ch == CHUNKS - 1:
            send_up(0, q.at[0], (1.0, 1.0))

    def build_coef(b):
        edge = incoming(ITERS, b)
        base = b * block
        south_face = face(vk[base + 1, 0], vk[base + 2, 0], vk[base + 1, 1], vk[base + 2, 1])
        for i in range(block):
            r = base + i
            u, k = uk[r, 0], uk[r, 1]
            hu, hk = turn(edge, 2 * i), turn(edge, 2 * i + 1)
            me, ae, be, ne = face(
                u, pltpu.roll(jnp.where(first, hu, u), 127, 1),
                k, pltpu.roll(jnp.where(first, hk, k), 127, 1),
            )
            mw, aw, bw, nw = face(
                pltpu.roll(jnp.where(last, hu, u), 1, 1), u,
                pltpu.roll(jnp.where(last, hk, k), 1, 1), k,
            )
            ms, as_, bs, ns = south_face
            north_face = face(vk[r + 2, 0], vk[r + 3, 0], k, vk[r + 3, 1])
            mn, an, bn, nn = north_face
            wet = jnp.where(level < dep_v[pl.ds(r, 1), :], 1.0, 0.0)
            coef[r, 0] = mw
            coef[r, 1] = aw - me
            coef[r, 2] = nw - be
            coef[r, 3] = -ne
            coef[r, 4] = wet + (bw - ae) + (bs - an)
            coef[r, 5] = ms
            coef[r, 6] = as_ - mn
            coef[r, 7] = ns - bn
            coef[r, 8] = -nn
            south_face = north_face

    for ch in order:
        wait_lon(ITERS, ch)
        if ch == 0:
            wait_low(ITERS, vk)
        if ch == CHUNKS - 1:
            wait_high(ITERS, vk)
        over(ch, build_coef)

    def advance(k, b):
        edge = incoming(k, b)
        base = b * block
        window = [[q[k, base + j, c] for c in range(comps)] for j in range(4)]
        tiles = []
        for i in range(block):
            r = base + i
            window.append([q[k, r + 4, c] for c in range(comps)])
            w = [coef[r, j] for j in range(9)]
            for c in range(comps):
                s2, s1, mid, n1, n2 = (window[j][c] for j in range(5))
                halo = turn(edge, comps * i + c)
                new = (
                    (
                        w[0] * pltpu.roll(jnp.where(last_two, halo, mid), 2, 1)
                        + w[1] * pltpu.roll(jnp.where(last, halo, mid), 1, 1)
                    )
                    + (
                        w[2] * pltpu.roll(jnp.where(first, halo, mid), 127, 1)
                        + w[3] * pltpu.roll(jnp.where(first_two, halo, mid), 126, 1)
                    )
                    + ((w[5] * s2 + w[6] * s1) + (w[7] * n1 + w[8] * n2))
                    + w[4] * mid
                )
                if k < ITERS - 1:
                    q[k + 1, r + HALO, c] = new
                    tiles.append(new)
                else:
                    res[r, c] = new
            window.pop(0)
        if tiles:
            snd[k + 1, b] = pack_edges(tiles)

    stores = []
    for k in range(ITERS):
        for ch in order:
            wait_lon(k, ch)
            if ch == 0:
                wait_low(k, q.at[k])
            if ch == CHUNKS - 1:
                wait_high(k, q.at[k])
            over(ch, functools.partial(advance, k))
            if k < ITERS - 1:
                send_lon(k + 1, ch)
                if ch == 0:
                    send_down(k + 1, q.at[k + 1])
                if ch == CHUNKS - 1:
                    send_up(k + 1, q.at[k + 1], (1.0, 1.0))
            else:
                for c in range(comps):
                    for l in range(levels):
                        start, count = ch * per * block, per * block
                        copy = pltpu.make_async_copy(
                            res.at[pl.ds(start, count), c, l],
                            out.at[pl.ds((c * levels + l) * rows + start, count)],
                            out_sem.at[ch, c * levels + l],
                        )
                        copy.start()
                        stores.append(copy)

    wait_sends(ITERS, vk)
    for k in range(ITERS):
        wait_sends(k, q.at[k])
    for copy in stores:
        copy.wait()


def on_device(lons, lats, tracers, zonal_velocity, merid_velocity, diffusivity, depth):
    comps, levels, rows, cols = tracers.shape
    f32 = jnp.float32
    block = 32 // comps
    blocks = rows // block
    dma = pltpu.SemaphoreType.DMA
    result = pl.pallas_call(
        functools.partial(kernel, lons, lats, rows, levels, comps),
        out_shape=jax.ShapeDtypeStruct((comps * levels * rows, cols), f32),
        in_specs=[pl.BlockSpec(memory_space=pl.ANY)] * 5,
        out_specs=pl.BlockSpec(memory_space=pl.ANY),
        scratch_shapes=[
            pltpu.VMEM((ITERS, rows + 2 * HALO, comps, levels, cols), f32),
            pltpu.VMEM((rows, 2, levels, cols), f32),
            pltpu.VMEM((rows + 2 * HALO, 2, levels, cols), f32),
            pltpu.VMEM((rows, 9, levels, cols), f32),
            pltpu.VMEM((ITERS + 1, blocks, levels, cols), f32),
            pltpu.VMEM((ITERS + 1, blocks, levels, cols), f32),
            pltpu.VMEM((ITERS + 1, blocks, levels, cols), f32),
            pltpu.VMEM((ITERS + 1, HALO, comps, levels, cols), f32),
            pltpu.VMEM((rows, comps, levels, cols), f32),
            pltpu.VMEM((rows, cols), f32),
            pltpu.VMEM((rows, cols), jnp.int32),
            dma((ITERS + 1, CHUNKS, 2)),
            dma((ITERS + 1, CHUNKS, 2)),
            dma((ITERS + 1, 2)),
            dma((ITERS + 1, 2)),
            dma((2 + (2 + comps) * levels,)),
            dma((CHUNKS, comps * levels)),
        ],
        compiler_params=pltpu.CompilerParams(
            collective_id=0, has_side_effects=True, vmem_limit_bytes=56 * 2**20
        ),
        cost_estimate=pl.CostEstimate(flops=60 * 10**6, bytes_accessed=8 * 10**6, transcendentals=0),
    )(
        tracers.reshape(comps * levels * rows, cols),
        zonal_velocity.reshape(levels * rows, cols),
        merid_velocity.reshape(levels * rows, cols),
        diffusivity,
        depth,
    )
    return result.reshape(comps, levels, rows, cols)


def solution(mesh):
    in_specs = (
        P(None, None, "lat", "lon"),
        P(None, "lat", "lon"),
        P(None, "lat", "lon"),
        P("lat", "lon"),
        P("lat", "lon"),
    )
    out_specs = P(None, None, "lat", "lon")
    return jax.shard_map(
        functools.partial(on_device, mesh.shape["lon"], mesh.shape["lat"]),
        mesh=mesh, in_specs=in_specs, out_specs=out_specs, check_vma=False,
    )
```
